32 devices in a mesh: league: 2 (over y), dp: 4 (over x, core), fsdp: 4 (over z).
Axes of the slice: x: 2, y: 2, z: 4, core: 2. Of those that a mesh axis runs over, the one named last changes fastest.
Arguments:
- tokens: bfloat16 [16384, 5120], P(('league', 'dp', 'fsdp')), parts along dimension 0, may hold values from -6 to 6
- value_cotangent: bfloat16 [16384, 1024], P(('league', 'dp', 'fsdp')), parts along dimension 0, may hold values from -6 to 6
- value_weight: bfloat16 [5120, 1024], P('fsdp'), may hold values from -0.078125 to 0.078125
- adapter_down: bfloat16 [8, 64, 5120], P('dp', None, 'fsdp'), may hold values from -0.078125 to 0.078125
- adapter_up: bfloat16 [8, 64, 1024], P('dp'), may hold values from -0.1875 to 0.1875
- tile_token_policy: int32 [128], P(('league', 'dp', 'fsdp')), parts along dimension 0, may hold values from 0 to 7
- tile_live_length: int32 [128], P(('league', 'dp', 'fsdp')), parts along dimension 0, may hold values from 1 to 128
Outputs:
- input_cotangent: bfloat16 [16384, 5120], P(('league', 'dp', 'fsdp')), parts along dimension 0
- grad_a: float32 [16, 64, 5120], P(('league', 'dp'), None, 'fsdp'), parts along dimension 0
- grad_b: float32 [16, 64, 1024], P(('league', 'dp')), parts along dimension 0
The draws below stay inside these ranges and needn't reach their ends.
There are 2 independent parts, one for each index of `league`. The reference program is written for one: setup_inputs(seed, part) draws one part's arguments, and reference() takes and returns one part's arrays. A program takes and returns all parts, laid end to end along the dimension named above; an argument that names none is the same for every part. Nothing has to cross between parts.
All inputs are finite; a program needn't handle non-finite values.
Results may differ from the reference program's by a relative error of at most 0.0032.
Values may be sent and summed in bfloat16 or wider, within the bound.
No kernel may reach another device: no remote copies, remote signals or barrier semaphores. Data moves between devices by JAX's collectives and lax.ppermute only.
A program may use at most 192 MiB of HBM per device.

```python
import math
import jax
import jax.numpy as jnp
import numpy as np
from jax import lax

MODEL_DIM = 5120
VALUE_WIDTH = 1024
ADAPTER_RANK = 64
POLICY_COUNT = 8
TILE = 128
TILES = 64
TOKENS = 8192


def set_ends(entries, rng, low, high):
    shape = entries.shape
    index_at = [jax.random.randint(jax.random.fold_in(rng, axis), (), 0, shape[axis]) for axis in range(len(shape))]
    entries = entries.at[tuple(index_at)].set(low)
    longest = shape.index(max(shape))
    index_at[longest] = (index_at[longest] + 1) % shape[longest]
    return entries.at[tuple(index_at)].set(high)


def spiked(result, key, source, target, parts, factor):
    def block_of(dim):
        return (jnp.arange(result.shape[dim]) // (result.shape[dim] // parts)).reshape((-1,) + (1,) * (result.ndim - 1 - dim))

    near = jax.random.permutation(key, parts)[block_of(target)]
    other_side = (block_of(target) + parts // 2) % parts
    return jnp.where((block_of(source) == near) | (block_of(source) == other_side), factor * result, result)


def block_scale(rng, shape, shards, least, top_value):
    loudness, own = 1.0, jax.random.fold_in(rng, 6)
    for position, parts in shards:
        draws = jnp.exp(jax.random.uniform(jax.random.fold_in(own, position), (parts,), jnp.float32, least / len(shards), top_value / len(shards)))
        loudness = loudness * jnp.repeat(draws, shape[position] // parts).reshape([-1 if axis == position else 1 for axis in range(len(shape))])
    return loudness


def rank_table(count, skew):
    weights = [(1 << 20) // math.isqrt(rank ** skew) + 1 for rank in range(1, count + 1)]
    spread = 1 + sum(weights) // (1 << 30)
    return np.cumsum(np.array([max(1, weight // spread) for weight in weights]))


def skewed_ids(stream_key, dims, count, lean):
    grid = rank_table(count, lean)
    pick = jax.random.randint(jax.random.fold_in(stream_key, 1), dims, 0, int(grid[count - 1]))
    standing = jnp.searchsorted(jnp.asarray(grid, jnp.int32), pick, side="right")
    return jax.random.permutation(jax.random.fold_in(stream_key, 2), count)[standing].astype(jnp.int32)


def bell_draw(rng, extent, width, limit, cuts=(), kind=jnp.bfloat16):
    loudness = block_scale(rng, extent, cuts, -0.22, 0.18) if cuts else 1.0
    drawn = jax.random.normal(rng, extent, jnp.float32) * width * loudness
    return jnp.minimum(jnp.maximum(drawn, -limit), limit).astype(kind)


def heavy_noise(rng, dims, deviation, bound, split, heavy, kind=jnp.bfloat16):
    array = deviation * jax.random.normal(rng, dims, jnp.float32)
    if split:
        array = array * block_scale(rng, dims, split, -0.22, 0.18)
    return jnp.clip(spiked(array, jax.random.fold_in(rng, 3), *heavy), -bound, bound).astype(kind)


def setup_inputs(seed: int = 0, part: int = 0) -> dict:
    key_list = jax.random.split(jax.random.key(seed), 8)
    own_keys = jax.random.split(jax.random.fold_in(key_list[7], part), 8)
    tokens = heavy_noise(own_keys[0], (TOKENS, MODEL_DIM), 1.0, 6.0, ((0, 16),), (0, 1, 16, 2.0))
    value_cotangent = bell_draw(own_keys[1], (TOKENS, VALUE_WIDTH), 1.0, 6.0, ((0, 16),))
    value_weight = bell_draw(key_list[2], (MODEL_DIM, VALUE_WIDTH), MODEL_DIM ** -0.5, 0.078125, ((0, 4),))
    adapter_down = bell_draw(key_list[3], (POLICY_COUNT, ADAPTER_RANK, MODEL_DIM), MODEL_DIM ** -0.5, 0.078125, ((0, 4), (2, 4)))
    adapter_up = bell_draw(key_list[4], (POLICY_COUNT, ADAPTER_RANK, VALUE_WIDTH), VALUE_WIDTH ** -0.5, 0.1875, ((0, 4),))
    tile_token_policy = set_ends(skewed_ids(own_keys[5], (TILES,), POLICY_COUNT, 2), jax.random.fold_in(own_keys[5], 3), 0, POLICY_COUNT - 1).astype(jnp.int32)
    tile_live_length = set_ends(jax.random.randint(own_keys[6], (TILES,), 1, TILE + 1), jax.random.fold_in(own_keys[6], 1), 1, TILE).astype(jnp.int32)
    return {"tokens": tokens, "value_cotangent": value_cotangent, "value_weight": value_weight, "adapter_down": adapter_down, "adapter_up": adapter_up, "tile_token_policy": tile_token_policy, "tile_live_length": tile_live_length}


adapter_scale = 2.0

def reference(tokens, value_cotangent, value_weight, adapter_down, adapter_up, tile_token_policy, tile_live_length):
    row_index = jnp.arange(TILE, dtype=jnp.int32)
    live_mask = row_index[None, :] < tile_live_length[:, None]
    masked = jnp.where(live_mask[:, :, None], value_cotangent.reshape(TILES, TILE, VALUE_WIDTH), jnp.zeros((), value_cotangent.dtype))
    x_tiles = tokens.reshape(TILES, TILE, MODEL_DIM)

    def tile_step(carried, inputs):
        down_accumulator, up_accumulator = carried
        x_tile, value_grad_tile, policy_index = inputs
        down_matrix = lax.dynamic_index_in_dim(adapter_down, policy_index, 0, keepdims=False)
        up_matrix = lax.dynamic_index_in_dim(adapter_up, policy_index, 0, keepdims=False)
        frozen_contribution = jnp.dot(value_grad_tile, value_weight.T, preferred_element_type=jnp.float32)
        rank_activations = (adapter_scale * jnp.dot(value_grad_tile, up_matrix.T, preferred_element_type=jnp.float32)).astype(jnp.bfloat16)
        adapter_contribution = jnp.dot(rank_activations, down_matrix, preferred_element_type=jnp.float32)
        input_grad_tile = (frozen_contribution + adapter_contribution).astype(jnp.bfloat16)
        projected_rows = jnp.dot(x_tile, down_matrix.T, preferred_element_type=jnp.float32).astype(jnp.bfloat16)
        down_accumulator = down_accumulator.at[policy_index].add(jnp.dot(rank_activations.T, x_tile, preferred_element_type=jnp.float32))
        up_accumulator = up_accumulator.at[policy_index].add(adapter_scale * jnp.dot(projected_rows.T, value_grad_tile, preferred_element_type=jnp.float32))
        return ((down_accumulator, up_accumulator), input_grad_tile)
    initial = (jnp.zeros((POLICY_COUNT, ADAPTER_RANK, MODEL_DIM), jnp.float32), jnp.zeros((POLICY_COUNT, ADAPTER_RANK, VALUE_WIDTH), jnp.float32))
    (down_accumulator, up_accumulator), input_cotangent = lax.scan(tile_step, initial, (x_tiles, masked, tile_token_policy))
    normalizer = 1.0 / math.sqrt(TOKENS)
    return (input_cotangent.reshape(TOKENS, MODEL_DIM), down_accumulator * normalizer, up_accumulator * normalizer)
```

```python
import math

import jax
import jax.numpy as jnp
from jax import lax
from jax.sharding import Mesh
from jax.sharding import PartitionSpec as P

adapter_scale = 2.0
cores = 2


def shift(value, axis, by):
    size = lax.axis_size(axis)
    return lax.ppermute(value, axis, [(i, (i + by) % size) for i in range(size)])


def gather_steps(value, axis):
    blocks = [value]
    for _ in range(lax.axis_size(axis) - 1):
        blocks.append(shift(blocks[-1], axis, 1))
    return blocks


def body(tokens, value_cotangent, value_weight, adapter_down, adapter_up, tile_token_policy, tile_live_length):
    y_size, x_size, c_size, z_size = (lax.axis_size(a) for a in ("league", "x", "core", "fsdp"))
    y, x, c, z = (lax.axis_index(a) for a in ("league", "x", "core", "fsdp"))
    rows, width = tokens.shape
    kv = value_cotangent.shape[1]
    tiles = tile_token_policy.shape[0]
    tile_rows = rows // tiles
    own_policies, rank, cols = adapter_down.shape
    half = own_policies * rank // y_size
    slices = y_size * x_size * c_size
    depth = kv // slices
    bf16, f32 = jnp.bfloat16, jnp.float32

    live = jnp.arange(tile_rows, dtype=jnp.int32)[None, :] < tile_live_length[:, None]
    live = live.reshape(rows, 1)
    masked = jnp.where(live, value_cotangent, jnp.zeros((), bf16))

    down_share = lax.dynamic_slice_in_dim(adapter_down.reshape(own_policies * rank, cols), y * half, half, 0)
    up_rows = adapter_up.reshape(y_size, half, kv)
    up_rows = jnp.stack([lax.dynamic_index_in_dim(up_rows, (y - s) % y_size, 0, False) for s in range(y_size)])
    up_x = jnp.stack(gather_steps(up_rows, "x"))
    up_all = jnp.stack(gather_steps(up_x, "core"))

    down_z = jnp.stack(gather_steps(down_share, "fsdp"))
    down_x = jnp.stack(gather_steps(down_z, "x"))
    down_y = jnp.stack(gather_steps(down_x, "league"))
    down_all = jnp.stack(gather_steps(down_y, "core"))

    back_c = (c - jnp.arange(c_size)) % c_size
    back_x = (x - jnp.arange(x_size)) % x_size
    back_y = (y - jnp.arange(y_size)) % y_size
    first_row = ((back_x[None, :, None] * c_size + back_c[:, None, None]) * y_size + back_y[None, None, :]) * half
    row_policy = (first_row[..., None] + jnp.arange(half)) // rank
    token_policy = jnp.repeat(tile_token_policy, tile_rows)[:, None]
    mine = token_policy == row_policy.reshape(1, -1)

    all_rows = slices * half
    low_rank = adapter_scale * jnp.einsum(
        "tk,rk->tr", masked, up_all.reshape(all_rows, kv), preferred_element_type=f32
    )
    low_rank = jnp.where(mine, low_rank, 0.0).astype(bf16)

    lr = low_rank.reshape(rows, c_size, all_rows // c_size)
    kept = jnp.einsum("tr,td->rd", lr[:, 0], tokens, preferred_element_type=f32)
    for s in range(1, c_size):
        part = jnp.einsum("tr,td->rd", lr[:, s], tokens, preferred_element_type=f32).astype(bf16)
        kept = kept + shift(part, "core", -s).astype(f32)
    kept = kept.reshape(x_size, y_size * half, width)
    own = kept[0]
    for s in range(1, x_size):
        own = own + shift(kept[s].astype(bf16), "x", -s).astype(f32)
    own = own.reshape(y_size * half, z_size, cols).swapaxes(0, 1).astype(bf16)
    parts_a = lax.all_to_all(own, "fsdp", split_axis=0, concat_axis=0, tiled=True)
    normalizer = 1.0 / math.sqrt(rows * x_size * c_size * z_size)
    grad_a = jnp.sum(parts_a.astype(f32), axis=0) * normalizer

    order = "cyxzrd,tzd->tcxyr"
    tok = tokens.reshape(rows, z_size, cols)
    tok = jnp.stack([lax.dynamic_index_in_dim(tok, (z - s) % z_size, 1, False) for s in range(z_size)])
    down_k = down_all.transpose(3, 0, 2, 1, 4, 5).reshape(z_size, all_rows, cols)
    projected = sum(
        jnp.einsum("td,rd->tr", tok[s], down_k[s], preferred_element_type=f32) for s in range(z_size)
    )
    projected = jnp.where(mine, projected, 0.0).astype(bf16)
    pr = projected.reshape(rows, c_size, all_rows // c_size)
    kept = jnp.einsum("tr,tk->rk", pr[:, 0], masked, preferred_element_type=f32)
    for s in range(1, c_size):
        part = jnp.einsum("tr,tk->rk", pr[:, s], masked, preferred_element_type=f32).astype(bf16)
        kept = kept + shift(part, "core", -s).astype(f32)
    kept = kept.reshape(x_size, y_size * half, kv)
    own = kept[0]
    for s in range(1, x_size):
        own = own + shift(kept[s].astype(bf16), "x", -s).astype(f32)
    own = own.reshape(z_size, -1, kv).astype(bf16)
    parts_b = lax.all_to_all(own, "fsdp", split_axis=0, concat_axis=0, tiled=True)
    own_b = (jnp.sum(parts_b.astype(f32), axis=0) * (adapter_scale * normalizer)).astype(bf16)
    spread = jnp.broadcast_to(own_b[None], (z_size,) + own_b.shape)
    grad_b = lax.all_to_all(spread, "fsdp", split_axis=0, concat_axis=0, tiled=True).astype(f32)
    grad_b = grad_b.reshape(y_size * half, kv)

    def unroll(value):
        value = value.reshape(y_size, half, -1)
        value = jnp.stack([lax.dynamic_index_in_dim(value, (y - k) % y_size, 0, False) for k in range(y_size)])
        return value.reshape(own_policies, rank, -1)

    me = (x * c_size + c) * y_size + y
    weight_share = lax.dynamic_slice_in_dim(value_weight, me * depth, depth, 1).T
    own_weight = value_weight
    weight = []
    held = weight_share
    for s in range(z_size):
        if s:
            held = shift(held, "fsdp", 1)
            got = jnp.stack(gather_steps(held, "x"))
            got = jnp.stack(gather_steps(got, "league"))
            got = jnp.stack(gather_steps(got, "core"))
            weight.append(got.reshape(kv, cols))
    order_k = [
        (((x - dx) % x_size) * c_size + (c - dc) % c_size) * y_size + (y - dy) % y_size
        for dc in range(c_size)
        for dy in range(y_size)
        for dx in range(x_size)
    ]
    masked_k = jnp.concatenate([lax.dynamic_slice_in_dim(masked, k * depth, depth, 1) for k in order_k], axis=1)
    out = jnp.zeros((rows, width), bf16)
    for s in range(z_size):
        if s == 0:
            block = jnp.einsum("tk,dk->td", masked, value_weight, preferred_element_type=f32)
        else:
            block = jnp.dot(masked_k, weight[s - 1], preferred_element_type=f32)
        block = block + jnp.dot(low_rank, down_k[s], preferred_element_type=f32)
        out = lax.dynamic_update_slice_in_dim(out, block.astype(bf16), ((z - s) % z_size) * cols, 1)
    return out, unroll(grad_a), unroll(grad_b)


def solution(mesh):
    league, dp, fsdp = mesh.devices.shape
    fine = Mesh(mesh.devices.reshape(league, dp // cores, cores, fsdp), ("league", "x", "core", "fsdp"))
    every = ("league", "x", "core", "fsdp")
    return jax.shard_map(
        body,
        mesh=fine,
        in_specs=(
            P(every, None),
            P(every, None),
            P("fsdp", None),
            P(("x", "core"), None, "fsdp"),
            P(("x", "core"), None, None),
            P(every),
            P(every),
        ),
        out_specs=(
            P(every, None),
            P(("league", "x", "core"), None, "fsdp"),
            P(("league", "x", "core"), None, None),
        ),
        check_vma=False,
    )
```

```python
import functools
import math

import jax
import jax.numpy as jnp
from jax import lax
from jax.experimental import pallas as pl
from jax.experimental.pallas import tpu as pltpu
from jax.sharding import Mesh
from jax.sharding import PartitionSpec as P

adapter_scale = 2.0
cores = 2
bf16, f32 = jnp.bfloat16, jnp.float32
vmem_bytes = 40 * 1024 * 1024
nt = (((1,), (1,)), ((), ()))


def shift(value, axis, by):
    size = lax.axis_size(axis)
    return lax.ppermute(value, axis, [(i, (i + by) % size) for i in range(size)])


def gather_steps(value, axis):
    blocks = [value]
    for _ in range(lax.axis_size(axis) - 1):
        blocks.append(shift(blocks[-1], axis, 1))
    return blocks


def column_block(cols):
    for size in (640, 512, 384, 256, 128):
        if cols % size == 0:
            return size
    return cols


def column_spec(rows, cols, place):
    bc = column_block(cols)
    per = cols // bc
    if cols % 128 == 0:
        def index(*at):
            owner, block = place(*at)
            return 0, owner * per + block

        return pl.BlockSpec((rows, bc), index)

    def index(*at):
        owner, block = place(*at)
        return owner, 0, block

    return pl.BlockSpec((None, rows, bc), index)


def by_owner(value, cols):
    if cols % 128 == 0:
        return value
    return value.reshape(value.shape[0], -1, cols).swapaxes(0, 1)


def call(kernel, name, grid, in_specs, out_specs, out_shape, scratch, scalars, args, flops, aliases=None):
    moved = sum(math.prod(a.shape) * a.dtype.itemsize for a in args)
    return pl.pallas_call(
        kernel,
        grid_spec=pltpu.PrefetchScalarGridSpec(
            num_scalar_prefetch=len(scalars), grid=grid, in_specs=in_specs, out_specs=out_specs, scratch_shapes=scratch
        ),
        out_shape=out_shape,
        compiler_params=pltpu.CompilerParams(vmem_limit_bytes=vmem_bytes),
        cost_estimate=pl.CostEstimate(flops=flops, bytes_accessed=moved, transcendentals=0),
        input_output_aliases=aliases or {},
        name=name,
    )(*scalars, *args)


def whole(array):
    zeros = (0,) * array.ndim
    return pl.BlockSpec(array.shape, lambda *_: zeros)


def columns_policy(first, count, group, rank):
    parts = []
    for g in range(count):
        parts.append(first[g] + lax.broadcasted_iota(jnp.int32, (1, group), 1) // rank)
    return jnp.concatenate(parts, axis=1)


def low_rank_kernel(count, group, rank, first, policy, live, cot_ref, *refs):
    up_refs, (masked_ref, low_ref, low_t_ref) = refs[:count], refs[count:]
    tile = pl.program_id(0)
    rows, kv = cot_ref.shape
    keep = lax.broadcasted_iota(jnp.int32, (rows, kv), 0) < live[tile]
    masked = jnp.where(keep, cot_ref[...].astype(f32), 0.0).astype(bf16)
    masked_ref[...] = masked
    up = jnp.concatenate([r[...] for r in up_refs], axis=0)
    low = adapter_scale * lax.dot_general(masked, up, nt, preferred_element_type=f32)
    mine = columns_policy(first, count, group, rank) == policy[tile]
    low = jnp.where(mine, low, 0.0)
    low_ref[...] = low.astype(bf16)
    low_t_ref[...] = low.T.astype(bf16)


def low_rank_call(first, policy, live, cotangent, ups, rank):
    rows, kv = cotangent.shape
    tiles = policy.shape[0]
    group = ups[0].shape[0]
    total = group * len(ups)
    tile_rows = rows // tiles
    return call(
        functools.partial(low_rank_kernel, len(ups), group, rank),
        "low_rank",
        (tiles,),
        [pl.BlockSpec((tile_rows, kv), lambda i, *_: (i, 0))] + [whole(u) for u in ups],
        [
            pl.BlockSpec((tile_rows, kv), lambda i, *_: (i, 0)),
            pl.BlockSpec((tile_rows, total), lambda i, *_: (i, 0)),
            pl.BlockSpec((total, tile_rows), lambda i, *_: (0, i)),
        ],
        [
            jax.ShapeDtypeStruct((rows, kv), bf16),
            jax.ShapeDtypeStruct((rows, total), bf16),
            jax.ShapeDtypeStruct((total, rows), bf16),
        ],
        [],
        (first, policy, live),
        [cotangent, *ups],
        2 * rows * kv * total,
    )


def partial_kernel(adds, blocks, low_t_ref, tok_ref, *refs):
    value = jnp.dot(low_t_ref[...], tok_ref[...], preferred_element_type=f32)
    if adds:
        value = value + refs[0][0].astype(f32)
    refs[-1][0] = value.astype(refs[-1].dtype)


def partial_call(low_t, tokens, blocks, cols, added, dtype):
    rows = low_t.shape[0]
    count = blocks.shape[0]
    bc = column_block(cols)
    per = cols // bc
    in_specs = [whole(low_t), column_spec(low_t.shape[1], cols, lambda i, j, b: (b[i], j))]
    args = [low_t, tokens]
    if added is not None:
        in_specs.append(pl.BlockSpec((1, rows, bc), lambda i, j, b: (i, 0, j)))
        args.append(added)
    return call(
        functools.partial(partial_kernel, added is not None),
        "down_partial",
        (count, per),
        in_specs,
        pl.BlockSpec((1, rows, bc), lambda i, j, b: (i, 0, j)),
        jax.ShapeDtypeStruct((count, rows, cols), dtype),
        [],
        (blocks,),
        args,
        2 * rows * low_t.shape[1] * cols * count,
    )


def place_down(store, refs, half, back, scalars, at):
    y_size = len(back)
    for n, ref in enumerate(refs):
        g, s = divmod(n, y_size)
        row = pl.multiple_of(scalars[at + s] * half, half) + g * y_size * half
        store[pl.ds(row, half), :] = ref[0]


def projected_first_kernel(count, blocks, tok_ref, *refs):
    out_ref = refs[-1]
    down = jnp.concatenate([r[...] for r in refs[:count]], axis=0)

    @pl.when(pl.program_id(0) == 0)
    def _():
        out_ref[...] = jnp.zeros_like(out_ref)

    out_ref[...] += lax.dot_general(tok_ref[...], down, nt, preferred_element_type=f32)


def projected_first(tokens, downs, blocks, rows):
    group, cols = downs[0].shape
    total = group * len(downs)
    bc = column_block(cols)
    per = cols // bc
    return call(
        functools.partial(projected_first_kernel, len(downs)),
        "projected_own",
        (per,),
        [column_spec(rows, cols, lambda j, b: (b[0], j))]
        + [pl.BlockSpec((group, bc), lambda j, b: (0, j)) for _ in downs],
        pl.BlockSpec((rows, total), lambda j, b: (0, 0)),
        jax.ShapeDtypeStruct((rows, total), f32),
        [],
        (blocks,),
        [tokens, *downs],
        2 * rows * cols * total,
    )


def projected_kernel(pieces, y_size, half, tiles, rank, split, scalars, first, policy, tok_ref, base_ref, masked_ref, *refs):
    piece_refs, (send_ref, keep_ref, store, total) = refs[:pieces], refs[pieces:]
    step = pl.program_id(0) * pl.num_programs(1) + pl.program_id(1)

    @pl.when(step == 0)
    def _():
        total[...] = base_ref[...]

    place_down(store, piece_refs, half, range(y_size), scalars, 0)
    total[...] += lax.dot_general(tok_ref[...], store[...], nt, preferred_element_type=f32)

    @pl.when(step == pl.num_programs(0) * pl.num_programs(1) - 1)
    def _():
        count = pieces // y_size
        columns = columns_policy(first, count, half * y_size, rank)
        tile_rows = total.shape[0] // tiles
        chosen = []
        for i in range(tiles):
            part = total[i * tile_rows : (i + 1) * tile_rows, :]
            chosen.append(jnp.where(columns == policy[i], part, 0.0).T)
        projected = jnp.concatenate(chosen, axis=1).astype(bf16)
        value = jnp.dot(projected, masked_ref[...], preferred_element_type=f32)
        keep_ref[...] = value[:split]
        send_ref[...] = value[split:]


def projected_call(scalars, first, policy, blocks_at, tokens, base, masked, pieces, y_size, half, rank, split):
    rows, kv = masked.shape
    steps, _, cols = pieces[0].shape
    total = half * len(pieces)
    bc = column_block(cols)
    per = cols // bc
    return call(
        functools.partial(projected_kernel, len(pieces), y_size, half, policy.shape[0], rank, split),
        "projected",
        (steps, per),
        [
            column_spec(rows, cols, lambda i, j, s, *_: (s[blocks_at + i], j)),
            whole(base),
            whole(masked),
        ]
        + [pl.BlockSpec((1, half, bc), lambda i, j, *_: (i, 0, j)) for _ in pieces],
        [
            pl.BlockSpec((total - split, kv), lambda *_: (0, 0)),
            pl.BlockSpec((split, kv), lambda *_: (0, 0)),
        ],
        [jax.ShapeDtypeStruct((total - split, kv), f32), jax.ShapeDtypeStruct((split, kv), f32)],
        [pltpu.VMEM((total, bc), bf16), pltpu.VMEM((rows, total), f32)],
        (scalars, first, policy),
        [tokens, base, masked, *pieces],
        2 * rows * cols * steps * total + 2 * rows * kv * total,
    )


def input_kernel(views, pieces, y_size, half, has_out, scalars, low_ref, *refs):
    masked_refs, refs = refs[:views], refs[views:]
    weight_refs, refs = refs[:views], refs[views:]
    down_refs, refs = refs[:pieces], refs[pieces:]
    if has_out:
        refs = refs[1:]
    out_ref = refs[0]
    masked = jnp.concatenate([r[...] for r in masked_refs], axis=1)
    weight = jnp.concatenate([r[...] for r in weight_refs], axis=1)
    value = lax.dot_general(masked, weight, nt, preferred_element_type=f32)
    if y_size:
        place_down(refs[1], down_refs, half, range(y_size), scalars, 1 + views)
        down = refs[1][...]
    else:
        down = jnp.concatenate([r[...] for r in down_refs], axis=0)
    value = value + jnp.dot(low_ref[...], down, preferred_element_type=f32)
    out_ref[...] = value.astype(bf16)


def input_call(scalars, low, masked, weights, downs, step, y_size, out, width):
    rows, kv = masked.shape
    cols = weights[0].shape[0]
    depth = weights[0].shape[1]
    half = downs[0].shape[-2]
    total = low.shape[1]
    bc = column_block(cols)
    per = cols // bc
    if y_size:
        down_specs = [pl.BlockSpec((1, half, bc), lambda j, s: (step, 0, j)) for _ in downs]
    else:
        down_specs = [pl.BlockSpec((half, bc), lambda j, s: (0, j)) for _ in downs]
    in_specs = [whole(low)]
    for v in range(len(weights)):
        in_specs.append(pl.BlockSpec((rows, depth), functools.partial(lambda v, j, s: (0, s[1 + v]), v)))
    in_specs += [pl.BlockSpec((bc, depth), lambda j, s: (j, 0)) for _ in weights] + down_specs
    args = [low] + [masked] * len(weights) + list(weights) + list(downs)
    aliases = {}
    if out is not None:
        in_specs.append(pl.BlockSpec(memory_space=pl.ANY))
        aliases = {1 + len(args): 0}
        args.append(out)
    return call(
        functools.partial(input_kernel, len(weights), len(downs), y_size, half, out is not None),
        "input_cotangent",
        (per,),
        in_specs,
        column_spec(rows, cols, lambda j, s: (s[0], j)),
        jax.ShapeDtypeStruct((rows, width) if cols % 128 == 0 else (width // cols, rows, cols), bf16),
        [pltpu.VMEM((total, bc), bf16)] if y_size else [],
        (scalars,),
        args,
        2 * rows * cols * (kv + total),
        aliases,
    )


def body(tokens, value_cotangent, value_weight, adapter_down, adapter_up, tile_token_policy, tile_live_length):
    y_size, x_size, c_size, z_size = (lax.axis_size(a) for a in ("league", "x", "core", "fsdp"))
    y, x, c, z = (lax.axis_index(a) for a in ("league", "x", "core", "fsdp"))
    rows, width = tokens.shape
    kv = value_cotangent.shape[1]
    own_policies, rank, cols = adapter_down.shape
    group = own_policies * rank
    half = group // y_size
    depth = kv // (y_size * c_size)

    def ints(*values):
        return jnp.stack([jnp.asarray(v, jnp.int32) for v in values])

    up_x = gather_steps(adapter_up.reshape(group, kv), "x")
    ups = [piece for s in zip(*[gather_steps(u, "core") for u in up_x]) for piece in s]
    groups = [(dc, dx) for dc in range(c_size) for dx in range(x_size)]
    first = ints(*[(((x - dx) % x_size) * c_size + (c - dc) % c_size) * own_policies for dc, dx in groups])

    own_down = adapter_down.reshape(group, cols)
    down_x = gather_steps(own_down, "x")
    own_downs = [piece for s in zip(*[gather_steps(u, "core") for u in down_x]) for piece in s]
    down_half = lax.dynamic_slice_in_dim(own_down, y * half, half, 0)
    down_z = jnp.stack([shift(down_half, "fsdp", s) for s in range(1, z_size)])
    down_pieces = {}
    for dx, piece in enumerate(gather_steps(down_z, "x")):
        for dy, got in enumerate(gather_steps(piece, "league")):
            for dc, last in enumerate(gather_steps(got, "core")):
                down_pieces[dc, dx, dy] = last
    downs = [down_pieces[dc, dx, dy] for dc, dx in groups for dy in range(y_size)]
    league_back = [(y - s) % y_size for s in range(y_size)]

    masked, low, low_t = low_rank_call(first, tile_token_policy, tile_live_length, value_cotangent, ups, rank)

    tokens = by_owner(tokens, cols)

    split = x_size * group
    normalizer = 1.0 / math.sqrt(rows * x_size * c_size * z_size)
    order = [(z + s) % z_size for s in range(z_size)]
    chunks = [list(range(z_size // 2, z_size)), list(range(z_size // 2))]
    got_a = []
    for chunk in chunks:
        places = ints(*[order[s] for s in chunk])
        sent = [
            shift(partial_call(low_t[s * split : (s + 1) * split], tokens, places, cols, None, bf16), "core", -s)
            for s in range(1, c_size)
        ]
        added = sent[0] if len(sent) == 1 else sum(v.astype(f32) for v in sent)
        for_x = [
            shift(partial_call(low_t[s * group : (s + 1) * group], tokens, places, cols, added[:, s * group : (s + 1) * group], bf16), "x", -s)
            for s in range(1, x_size)
        ]
        kept = partial_call(low_t[:group], tokens, places, cols, added[:, :group], f32)
        for value in for_x:
            kept = kept + value.astype(f32)
        for n, s in enumerate(chunk):
            got_a.append(shift(kept[n].astype(bf16), "fsdp", s).astype(f32) if s else kept[n])
    grad_a = sum(got_a[1:], got_a[0]) * normalizer

    blocks = ints(*[(z - s) % z_size for s in range(z_size)])
    base = projected_first(tokens, own_downs, blocks, rows)
    scalars = jnp.concatenate([ints(*league_back), blocks[1:]])
    sent_b, kept_b = projected_call(
        scalars, first, tile_token_policy, y_size, tokens, base, masked, downs, y_size, half, rank, split
    )
    for s in range(1, c_size):
        kept_b = kept_b + shift(sent_b[(s - 1) * split : s * split], "core", -s)
    kept_b = kept_b.reshape(x_size, group, kv)
    own_b = kept_b[0]
    for s in range(1, x_size):
        own_b = own_b + shift(kept_b[s].astype(bf16), "x", -s).astype(f32)
    own_b = own_b.reshape(z_size, -1, kv).astype(bf16)
    parts_b = lax.all_to_all(own_b, "fsdp", split_axis=0, concat_axis=0, tiled=True)
    share_b = (jnp.sum(parts_b.astype(f32), axis=0) * (adapter_scale * normalizer)).astype(bf16)
    spread = jnp.broadcast_to(share_b[None], (z_size,) + share_b.shape)
    grad_b = lax.all_to_all(spread, "fsdp", split_axis=0, concat_axis=0, tiled=True).astype(f32)

    out = input_call(ints(z, 0), low, masked, [value_weight], own_downs, 0, 0, None, width)
    held = lax.dynamic_slice_in_dim(value_weight, (y * c_size + c) * depth, depth, 1)
    for s in range(1, z_size):
        held = shift(held, "fsdp", 1)
        weights, places = [], []
        for dy, piece in enumerate(gather_steps(held, "league")):
            for dc, got in enumerate(gather_steps(piece, "core")):
                weights.append(got)
                places.append(league_back[dy] * c_size + (c - dc) % c_size)
        out = input_call(
            ints((z - s) % z_size, *places, *league_back), low, masked, weights, downs, s - 1, y_size, out, width
        )
    if cols % 128:
        out = out.swapaxes(0, 1).reshape(rows, width)
    return out, grad_a.reshape(own_policies, rank, cols), grad_b.reshape(own_policies, rank, kv)


def solution(mesh):
    league, dp, fsdp = mesh.devices.shape
    fine = Mesh(mesh.devices.reshape(league, dp // cores, cores, fsdp), ("league", "x", "core", "fsdp"))
    every = ("league", "x", "core", "fsdp")
    return jax.shard_map(
        body,
        mesh=fine,
        in_specs=(
            P(every, None),
            P(every, None),
            P("fsdp", None),
            P(("x", "core"), None, "fsdp"),
            P(("x", "core"), None, None),
            P(every),
            P(every),
        ),
        out_specs=(
            P(every, None),
            P(("league", "x", "core"), None, "fsdp"),
            P(("league", "x", "core"), None, None),
        ),
        check_vma=False,
    )
```

```python
import functools
import math

import jax
import jax.numpy as jnp
from jax import lax
from jax.experimental import pallas as pl
from jax.experimental.pallas import tpu as pltpu
from jax.sharding import Mesh
from jax.sharding import PartitionSpec as P

adapter_scale = 2.0
cores = 2
bf16, f32 = jnp.bfloat16, jnp.float32
vmem_bytes = 16 * 1024 * 1024
cost_factor = 20
nt = (((1,), (1,)), ((), ()))


def shift(value, axis, by):
    size = lax.axis_size(axis)
    return lax.ppermute(value, axis, [(i, (i + by) % size) for i in range(size)])


def gather_steps(value, axis):
    blocks = [value]
    for _ in range(lax.axis_size(axis) - 1):
        blocks.append(shift(blocks[-1], axis, 1))
    return blocks


def column_block(cols):
    for size in (640, 512, 384, 256, 128):
        if cols % size == 0:
            return size
    return cols


def column_spec(rows, cols, place):
    bc = column_block(cols)
    per = cols // bc
    if cols % 128 == 0:
        def index(*at):
            owner, block = place(*at)
            return 0, owner * per + block

        return pl.BlockSpec((rows, bc), index)

    def index(*at):
        owner, block = place(*at)
        return owner, 0, block

    return pl.BlockSpec((None, rows, bc), index)


def by_owner(value, cols):
    if cols % 128 == 0:
        return value
    return value.reshape(value.shape[0], -1, cols).swapaxes(0, 1)


def call(kernel, name, grid, in_specs, out_specs, out_shape, scratch, scalars, args, flops, aliases=None, in_hbm=()):
    args = [pltpu.with_memory_space_constraint(a, pltpu.HBM) if n in in_hbm else a for n, a in enumerate(args)]
    moved = sum(math.prod(a.shape) * a.dtype.itemsize for a in args)
    return pl.pallas_call(
        kernel,
        grid_spec=pltpu.PrefetchScalarGridSpec(
            num_scalar_prefetch=len(scalars), grid=grid, in_specs=in_specs, out_specs=out_specs, scratch_shapes=scratch
        ),
        out_shape=out_shape,
        compiler_params=pltpu.CompilerParams(vmem_limit_bytes=vmem_bytes),
        cost_estimate=pl.CostEstimate(flops=cost_factor * flops, bytes_accessed=cost_factor * moved, transcendentals=0),
        input_output_aliases=aliases or {},
        name=name,
    )(*scalars, *args)


def whole(array):
    zeros = (0,) * array.ndim
    return pl.BlockSpec(array.shape, lambda *_: zeros)


def columns_policy(first, count, group, rank):
    parts = []
    for g in range(count):
        parts.append(first[g] + lax.broadcasted_iota(jnp.int32, (1, group), 1) // rank)
    return jnp.concatenate(parts, axis=1)


def low_rank_kernel(count, group, rank, first, policy, live, cot_ref, *refs):
    up_refs, (masked_ref, low_ref, low_t_ref) = refs[:count], refs[count:]
    tile = pl.program_id(0)
    rows, kv = cot_ref.shape
    keep = lax.broadcasted_iota(jnp.int32, (rows, kv), 0) < live[tile]
    masked = jnp.where(keep, cot_ref[...].astype(f32), 0.0).astype(bf16)
    masked_ref[...] = masked
    up = jnp.concatenate([r[...] for r in up_refs], axis=0)
    low = adapter_scale * lax.dot_general(masked, up, nt, preferred_element_type=f32)
    mine = columns_policy(first, count, group, rank) == policy[tile]
    low = jnp.where(mine, low, 0.0)
    low_ref[...] = low.astype(bf16)
    low_t_ref[...] = low.T.astype(bf16)


def low_rank_call(first, policy, live, cotangent, ups, rank):
    rows, kv = cotangent.shape
    tiles = policy.shape[0]
    group = ups[0].shape[0]
    total = group * len(ups)
    tile_rows = rows // tiles
    return call(
        functools.partial(low_rank_kernel, len(ups), group, rank),
        "low_rank",
        (tiles,),
        [pl.BlockSpec((tile_rows, kv), lambda i, *_: (i, 0))] + [whole(u) for u in ups],
        [
            pl.BlockSpec((tile_rows, kv), lambda i, *_: (i, 0)),
            pl.BlockSpec((tile_rows, total), lambda i, *_: (i, 0)),
            pl.BlockSpec((total, tile_rows), lambda i, *_: (0, i)),
        ],
        [
            jax.ShapeDtypeStruct((rows, kv), bf16),
            jax.ShapeDtypeStruct((rows, total), bf16),
            jax.ShapeDtypeStruct((total, rows), bf16),
        ],
        [],
        (first, policy, live),
        [cotangent, *ups],
        2 * rows * kv * total,
        in_hbm=(0,),
    )


def partial_kernel(adds, low_t_ref, tok_ref, *refs):
    value = jnp.dot(low_t_ref[...], tok_ref[...], preferred_element_type=f32)
    if adds:
        value = value + refs[0][0].astype(f32)
    at = 0
    for ref in refs[adds:]:
        ref[0] = value[at : at + ref.shape[1]].astype(ref.dtype)
        at += ref.shape[1]


def partial_call(low_t, first, rows, tokens, blocks, cols, added, kinds):
    count = blocks.shape[0]
    bc = column_block(cols)
    per = cols // bc
    depth = low_t.shape[1]
    in_specs = [
        pl.BlockSpec((rows, depth), lambda i, j, b: (first // rows, 0)),
        column_spec(depth, cols, lambda i, j, b: (b[i], j)),
    ]
    args = [low_t, tokens]
    if added is not None:
        in_specs.append(pl.BlockSpec((1, rows, bc), lambda i, j, b: (i, 0, j)))
        args.append(added)
    part = rows // len(kinds)
    return call(
        lambda b, *refs: partial_kernel(int(added is not None), *refs),
        "down_partial",
        (count, per),
        in_specs,
        [pl.BlockSpec((1, part, bc), lambda i, j, b: (i, 0, j)) for _ in kinds],
        [jax.ShapeDtypeStruct((count, part, cols), kind) for kind in kinds],
        [],
        (blocks,),
        args,
        2 * rows * depth * cols * count,
        in_hbm=(1,),
    )


def place_down(store, refs, half, back, scalars, at):
    y_size = len(back)
    for n, ref in enumerate(refs):
        g, s = divmod(n, y_size)
        row = pl.multiple_of(scalars[at + s] * half, half) + g * y_size * half
        store[pl.ds(row, half), :] = ref[0]


def projected_first_kernel(count, blocks, tok_ref, *refs):
    out_ref = refs[-1]
    down = jnp.concatenate([r[...] for r in refs[:count]], axis=0)

    @pl.when(pl.program_id(0) == 0)
    def _():
        out_ref[...] = jnp.zeros_like(out_ref)

    out_ref[...] += lax.dot_general(tok_ref[...], down, nt, preferred_element_type=f32)


def projected_first(tokens, downs, blocks, rows):
    group, cols = downs[0].shape
    total = group * len(downs)
    bc = column_block(cols)
    per = cols // bc
    return call(
        functools.partial(projected_first_kernel, len(downs)),
        "projected_own",
        (per,),
        [column_spec(rows, cols, lambda j, b: (b[0], j))]
        + [pl.BlockSpec((group, bc), lambda j, b: (0, j)) for _ in downs],
        pl.BlockSpec((rows, total), lambda j, b: (0, 0)),
        jax.ShapeDtypeStruct((rows, total), f32),
        [],
        (blocks,),
        [tokens, *downs],
        2 * rows * cols * total,
        in_hbm=(0,),
    )


def projected_kernel(pieces, y_size, half, tiles, rank, split, scalars, first, policy, tok_ref, base_ref, masked_ref, *refs):
    piece_refs, (send_ref, keep_ref, store, total) = refs[:pieces], refs[pieces:]
    step = pl.program_id(0) * pl.num_programs(1) + pl.program_id(1)

    @pl.when(step == 0)
    def _():
        total[...] = base_ref[...]

    place_down(store, piece_refs, half, range(y_size), scalars, 0)
    total[...] += lax.dot_general(tok_ref[...], store[...], nt, preferred_element_type=f32)

    @pl.when(step == pl.num_programs(0) * pl.num_programs(1) - 1)
    def _():
        count = pieces // y_size
        columns = columns_policy(first, count, half * y_size, rank)
        tile_rows = total.shape[0] // tiles
        chosen = []
        for i in range(tiles):
            part = total[i * tile_rows : (i + 1) * tile_rows, :]
            chosen.append(jnp.where(columns == policy[i], part, 0.0).T)
        projected = jnp.concatenate(chosen, axis=1).astype(bf16)
        value = jnp.dot(projected, masked_ref[...], preferred_element_type=f32)
        keep_ref[...] = value[:split]
        send_ref[...] = value[split:]


def projected_call(scalars, first, policy, blocks_at, tokens, base, masked, pieces, y_size, half, rank, split):
    rows, kv = masked.shape
    steps, _, cols = pieces[0].shape
    total = half * len(pieces)
    bc = column_block(cols)
    per = cols // bc
    return call(
        functools.partial(projected_kernel, len(pieces), y_size, half, policy.shape[0], rank, split),
        "projected",
        (steps, per),
        [
            column_spec(rows, cols, lambda i, j, s, *_: (s[blocks_at + i], j)),
            whole(base),
            whole(masked),
        ]
        + [pl.BlockSpec((1, half, bc), lambda i, j, *_: (i, 0, j)) for _ in pieces],
        [
            pl.BlockSpec((total - split, kv), lambda *_: (0, 0)),
            pl.BlockSpec((split, kv), lambda *_: (0, 0)),
        ],
        [jax.ShapeDtypeStruct((total - split, kv), f32), jax.ShapeDtypeStruct((split, kv), f32)],
        [pltpu.VMEM((total, bc), bf16), pltpu.VMEM((rows, total), f32)],
        (scalars, first, policy),
        [tokens, base, masked, *pieces],
        2 * rows * cols * steps * total + 2 * rows * kv * total,
        in_hbm=(0,),
    )


def input_kernel(views, pieces, y_size, half, has_out, scalars, low_ref, *refs):
    masked_refs, refs = refs[:views], refs[views:]
    weight_refs, refs = refs[:views], refs[views:]
    down_refs, refs = refs[:pieces], refs[pieces:]
    if has_out:
        refs = refs[1:]
    out_ref = refs[0]
    masked = jnp.concatenate([r[...] for r in masked_refs], axis=1)
    weight = jnp.concatenate([r[...] for r in weight_refs], axis=1)
    value = lax.dot_general(masked, weight, nt, preferred_element_type=f32)
    if y_size:
        place_down(refs[1], down_refs, half, range(y_size), scalars, 1 + views)
        down = refs[1][...]
    else:
        down = jnp.concatenate([r[...] for r in down_refs], axis=0)
    value = value + jnp.dot(low_ref[...], down, preferred_element_type=f32)
    out_ref[...] = value.astype(bf16)


def input_call(scalars, low, masked, weights, downs, step, y_size, out, width):
    rows, kv = masked.shape
    cols = weights[0].shape[0]
    depth = weights[0].shape[1]
    half = downs[0].shape[-2]
    total = low.shape[1]
    bc = column_block(cols)
    per = cols // bc
    if y_size:
        down_specs = [pl.BlockSpec((1, half, bc), lambda j, s: (step, 0, j)) for _ in downs]
    else:
        down_specs = [pl.BlockSpec((half, bc), lambda j, s: (0, j)) for _ in downs]
    in_specs = [whole(low)]
    for v in range(len(weights)):
        in_specs.append(pl.BlockSpec((rows, depth), functools.partial(lambda v, j, s: (0, s[1 + v]), v)))
    in_specs += [pl.BlockSpec((bc, depth), lambda j, s: (j, 0)) for _ in weights] + down_specs
    args = [low] + [masked] * len(weights) + list(weights) + list(downs)
    aliases = {}
    if out is not None:
        in_specs.append(pl.BlockSpec(memory_space=pl.ANY))
        aliases = {1 + len(args): 0}
        args.append(out)
    return call(
        functools.partial(input_kernel, len(weights), len(downs), y_size, half, out is not None),
        "input_cotangent",
        (per,),
        in_specs,
        column_spec(rows, cols, lambda j, s: (s[0], j)),
        jax.ShapeDtypeStruct((rows, width) if cols % 128 == 0 else (width // cols, rows, cols), bf16),
        [pltpu.VMEM((total, bc), bf16)] if y_size else [],
        (scalars,),
        args,
        2 * rows * cols * (kv + total),
        aliases,
        (1 + len(weights),) if not y_size else (),
    )


def body(tokens, value_cotangent, value_weight, adapter_down, adapter_up, tile_token_policy, tile_live_length):
    y_size, x_size, c_size, z_size = (lax.axis_size(a) for a in ("league", "x", "core", "fsdp"))
    y, x, c, z = (lax.axis_index(a) for a in ("league", "x", "core", "fsdp"))
    rows, width = tokens.shape
    kv = value_cotangent.shape[1]
    own_policies, rank, cols = adapter_down.shape
    group = own_policies * rank
    half = group // y_size
    depth = kv // (y_size * c_size)

    def ints(*values):
        return jnp.stack([jnp.asarray(v, jnp.int32) for v in values])

    up_x = gather_steps(adapter_up.reshape(group, kv), "x")
    ups = [piece for s in zip(*[gather_steps(u, "core") for u in up_x]) for piece in s]
    groups = [(dc, dx) for dc in range(c_size) for dx in range(x_size)]
    first = ints(*[(((x - dx) % x_size) * c_size + (c - dc) % c_size) * own_policies for dc, dx in groups])

    own_down = adapter_down.reshape(group, cols)
    down_x = gather_steps(own_down, "x")
    own_downs = [piece for s in zip(*[gather_steps(u, "core") for u in down_x]) for piece in s]
    down_half = lax.dynamic_slice_in_dim(own_down, y * half, half, 0)
    down_z = jnp.stack([shift(down_half, "fsdp", s) for s in range(1, z_size)])
    down_pieces = {}
    for dx, piece in enumerate(gather_steps(down_z, "x")):
        for dy, got in enumerate(gather_steps(piece, "league")):
            for dc, last in enumerate(gather_steps(got, "core")):
                down_pieces[dc, dx, dy] = last
    downs = [down_pieces[dc, dx, dy] for dc, dx in groups for dy in range(y_size)]
    league_back = [(y - s) % y_size for s in range(y_size)]

    masked, low, low_t = low_rank_call(first, tile_token_policy, tile_live_length, value_cotangent, ups, rank)

    tokens = by_owner(tokens, cols)

    split = x_size * group
    normalizer = 1.0 / math.sqrt(rows * x_size * c_size * z_size)
    order = [(z + s) % z_size for s in range(z_size)]
    chunks = [list(range(z_size // 2, z_size)), list(range(z_size // 2))]
    got_a = []
    for chunk in chunks:
        places = ints(*[order[s] for s in chunk])
        sent = [
            shift(partial_call(low_t, s * split, split, tokens, places, cols, None, [bf16])[0], "core", -s)
            for s in range(1, c_size)
        ]
        added = sent[0] if len(sent) == 1 else sum(v.astype(f32) for v in sent)
        kept, *for_x = partial_call(low_t, 0, split, tokens, places, cols, added, [f32] + [bf16] * (x_size - 1))
        for_x = [shift(v, "x", -s - 1) for s, v in enumerate(for_x)]
        for value in for_x:
            kept = kept + value.astype(f32)
        for n, s in enumerate(chunk):
            got_a.append(shift(kept[n].astype(bf16), "fsdp", s).astype(f32) if s else kept[n])
    grad_a = sum(got_a[1:], got_a[0]) * normalizer

    blocks = ints(*[(z - s) % z_size for s in range(z_size)])
    base = projected_first(tokens, own_downs, blocks, rows)
    scalars = jnp.concatenate([ints(*league_back), blocks[1:]])
    sent_b, kept_b = projected_call(
        scalars, first, tile_token_policy, y_size, tokens, base, masked, downs, y_size, half, rank, split
    )
    for s in range(1, c_size):
        kept_b = kept_b + shift(sent_b[(s - 1) * split : s * split], "core", -s)
    kept_b = kept_b.reshape(x_size, group, kv)
    own_b = kept_b[0]
    for s in range(1, x_size):
        own_b = own_b + shift(kept_b[s].astype(bf16), "x", -s).astype(f32)
    own_b = own_b.reshape(z_size, -1, kv).astype(bf16)
    parts_b = lax.all_to_all(own_b, "fsdp", split_axis=0, concat_axis=0, tiled=True)
    share_b = (jnp.sum(parts_b.astype(f32), axis=0) * (adapter_scale * normalizer)).astype(bf16)
    spread = jnp.broadcast_to(share_b[None], (z_size,) + share_b.shape)
    grad_b = lax.all_to_all(spread, "fsdp", split_axis=0, concat_axis=0, tiled=True).astype(f32)

    out = input_call(ints(z, 0), low, masked, [value_weight], own_downs, 0, 0, None, width)
    held = lax.dynamic_slice_in_dim(value_weight, (y * c_size + c) * depth, depth, 1)
    for s in range(1, z_size):
        held = shift(held, "fsdp", 1)
        weights, places = [], []
        for dy, piece in enumerate(gather_steps(held, "league")):
            for dc, got in enumerate(gather_steps(piece, "core")):
                weights.append(got)
                places.append(league_back[dy] * c_size + (c - dc) % c_size)
        out = input_call(
            ints((z - s) % z_size, *places, *league_back), low, masked, weights, downs, s - 1, y_size, out, width
        )
    if cols % 128:
        out = out.swapaxes(0, 1).reshape(rows, width)
    return out, grad_a.reshape(own_policies, rank, cols), grad_b.reshape(own_policies, rank, kv)


def solution(mesh):
    league, dp, fsdp = mesh.devices.shape
    fine = Mesh(mesh.devices.reshape(league, dp // cores, cores, fsdp), ("league", "x", "core", "fsdp"))
    every = ("league", "x", "core", "fsdp")
    return jax.shard_map(
        body,
        mesh=fine,
        in_specs=(
            P(every, None),
            P(every, None),
            P("fsdp", None),
            P(("x", "core"), None, "fsdp"),
            P(("x", "core"), None, None),
            P(every),
            P(every),
        ),
        out_specs=(
            P(every, None),
            P(("league", "x", "core"), None, "fsdp"),
            P(("league", "x", "core"), None, None),
        ),
        check_vma=False,
    )
```

```python
import functools
import math

import jax
import jax.numpy as jnp
from jax import lax
from jax.experimental import pallas as pl
from jax.experimental.pallas import tpu as pltpu
from jax.sharding import Mesh
from jax.sharding import PartitionSpec as P

adapter_scale = 2.0
cores = 2
bf16, f32 = jnp.bfloat16, jnp.float32
vmem_bytes = 16 * 1024 * 1024
cost_factor = 20
nt = (((1,), (1,)), ((), ()))


def shift(value, axis, by):
    size = lax.axis_size(axis)
    return lax.ppermute(value, axis, [(i, (i + by) % size) for i in range(size)])


def gather_steps(value, axis):
    blocks = [value]
    for _ in range(lax.axis_size(axis) - 1):
        blocks.append(shift(blocks[-1], axis, 1))
    return blocks


def column_block(cols):
    for size in (640, 512, 384, 256, 128):
        if cols % size == 0:
            return size
    return cols


def column_spec(rows, cols, place):
    bc = column_block(cols)
    per = cols // bc
    if cols % 128 == 0:
        def index(*at):
            owner, block = place(*at)
            return 0, owner * per + block

        return pl.BlockSpec((rows, bc), index)

    def index(*at):
        owner, block = place(*at)
        return owner, 0, block

    return pl.BlockSpec((None, rows, bc), index)


def by_owner(value, cols):
    if cols % 128 == 0:
        return value
    return value.reshape(value.shape[0], -1, cols).swapaxes(0, 1)


def call(kernel, name, grid, in_specs, out_specs, out_shape, scratch, scalars, args, flops, aliases=None, in_hbm=(), later_than=()):
    args = [pltpu.with_memory_space_constraint(a, pltpu.HBM) if n in in_hbm else a for n, a in enumerate(args)]
    moved = sum(math.prod(a.shape) * a.dtype.itemsize for a in args)
    count, extra = len(scalars) + len(args), len(later_than)
    return pl.pallas_call(
        lambda *refs: kernel(*refs[:count], *refs[count + extra :]),
        grid_spec=pltpu.PrefetchScalarGridSpec(
            num_scalar_prefetch=len(scalars), grid=grid, in_specs=in_specs + [pl.BlockSpec(memory_space=pl.ANY)] * extra, out_specs=out_specs, scratch_shapes=scratch
        ),
        out_shape=out_shape,
        compiler_params=pltpu.CompilerParams(vmem_limit_bytes=vmem_bytes),
        cost_estimate=pl.CostEstimate(flops=cost_factor * flops, bytes_accessed=cost_factor * moved, transcendentals=0),
        input_output_aliases=aliases or {},
        name=name,
    )(*scalars, *args, *later_than)


def whole(array):
    zeros = (0,) * array.ndim
    return pl.BlockSpec(array.shape, lambda *_: zeros)


def columns_policy(first, count, group, rank):
    parts = []
    for g in range(count):
        parts.append(first[g] + lax.broadcasted_iota(jnp.int32, (1, group), 1) // rank)
    return jnp.concatenate(parts, axis=1)


def low_rank_kernel(count, group, rank, first, policy, live, cot_ref, *refs):
    up_refs, (masked_ref, low_ref, low_t_ref) = refs[:count], refs[count:]
    tile = pl.program_id(0)
    rows, kv = cot_ref.shape
    keep = lax.broadcasted_iota(jnp.int32, (rows, kv), 0) < live[tile]
    masked = jnp.where(keep, cot_ref[...].astype(f32), 0.0).astype(bf16)
    masked_ref[...] = masked
    up = jnp.concatenate([r[...] for r in up_refs], axis=0)
    low = adapter_scale * lax.dot_general(masked, up, nt, preferred_element_type=f32)
    mine = columns_policy(first, count, group, rank) == policy[tile]
    low = jnp.where(mine, low, 0.0)
    low_ref[...] = low.astype(bf16)
    low_t_ref[...] = low.T.astype(bf16)


def low_rank_call(first, policy, live, cotangent, ups, rank):
    rows, kv = cotangent.shape
    tiles = policy.shape[0]
    group = ups[0].shape[0]
    total = group * len(ups)
    tile_rows = rows // tiles
    return call(
        functools.partial(low_rank_kernel, len(ups), group, rank),
        "low_rank",
        (tiles,),
        [pl.BlockSpec((tile_rows, kv), lambda i, *_: (i, 0))] + [whole(u) for u in ups],
        [
            pl.BlockSpec((tile_rows, kv), lambda i, *_: (i, 0)),
            pl.BlockSpec((tile_rows, total), lambda i, *_: (i, 0)),
            pl.BlockSpec((total, tile_rows), lambda i, *_: (0, i)),
        ],
        [
            jax.ShapeDtypeStruct((rows, kv), bf16),
            jax.ShapeDtypeStruct((rows, total), bf16),
            jax.ShapeDtypeStruct((total, rows), bf16),
        ],
        [],
        (first, policy, live),
        [cotangent, *ups],
        2 * rows * kv * total,
        in_hbm=(0,),
    )


def partial_kernel(adds, low_t_ref, tok_ref, *refs):
    value = jnp.dot(low_t_ref[...], tok_ref[...], preferred_element_type=f32)
    if adds:
        value = value + refs[0][0].astype(f32)
    at = 0
    for ref in refs[adds:]:
        ref[0] = value[at : at + ref.shape[1]].astype(ref.dtype)
        at += ref.shape[1]


def partial_call(low_t, first, rows, tokens, blocks, cols, added, kinds):
    count = blocks.shape[0]
    bc = column_block(cols)
    per = cols // bc
    depth = low_t.shape[1]
    in_specs = [
        pl.BlockSpec((rows, depth), lambda i, j, b: (first // rows, 0)),
        column_spec(depth, cols, lambda i, j, b: (b[i], j)),
    ]
    args = [low_t, tokens]
    if added is not None:
        in_specs.append(pl.BlockSpec((1, rows, bc), lambda i, j, b: (i, 0, j)))
        args.append(added)
    part = rows // len(kinds)
    return call(
        lambda b, *refs: partial_kernel(int(added is not None), *refs),
        "down_partial",
        (count, per),
        in_specs,
        [pl.BlockSpec((1, part, bc), lambda i, j, b: (i, 0, j)) for _ in kinds],
        [jax.ShapeDtypeStruct((count, part, cols), kind) for kind in kinds],
        [],
        (blocks,),
        args,
        2 * rows * depth * cols * count,
        in_hbm=(1,),
    )


def settle_kernel(kept_ref, *refs):
    count = kept_ref.shape[0]
    got_refs, out_refs = refs[:-count], refs[-count:]
    for m, out_ref in enumerate(out_refs):
        value = kept_ref[m]
        for ref in got_refs:
            value = value + ref[m].astype(f32)
        out_ref[...] = value.astype(out_ref.dtype)


def settle_call(kept, got, kinds, later_than):
    shapes = [jax.ShapeDtypeStruct(kept.shape[1:], kind) for kind in kinds]
    args = [kept, *got]
    specs = [whole(v) for v in args]
    outs = [whole(v) for v in shapes]
    return call(settle_kernel, "settle", (1,), specs, outs, shapes, [], (), args, 0, later_than=later_than)


def spread_kernel(group, x_at, kept_ref, *refs):
    out_ref = refs[-1]
    chunk = out_ref.shape[2]
    for s in range(out_ref.shape[0]):
        for m in range(out_ref.shape[1]):
            here = slice(s * group + m * chunk, s * group + (m + 1) * chunk)
            value = kept_ref[here, :]
            for ref in refs[:-1]:
                value = value + ref[here, :]
            out_ref[x_at[s], m] = value.astype(bf16)


def spread_call(x_at, kept, got, group, z_size):
    rows, kv = kept.shape
    shape = jax.ShapeDtypeStruct((rows // group, z_size, group // z_size, kv), bf16)
    args = [kept, *got]
    kernel = functools.partial(spread_kernel, group)
    return call(kernel, "spread", (1,), [whole(v) for v in args], whole(shape), shape, [], (x_at,), args, 0)


def share_kernel(scale, parts_ref, out_ref):
    value = parts_ref[0].astype(f32)
    for n in range(1, parts_ref.shape[0]):
        value = value + parts_ref[n].astype(f32)
    value = (value * scale).astype(bf16)
    for n in range(out_ref.shape[0]):
        out_ref[n] = value


def share_call(parts, scale, copies, later_than=()):
    shape = jax.ShapeDtypeStruct((copies,) + parts.shape[1:], bf16)
    kernel = functools.partial(share_kernel, scale)
    return call(kernel, "share", (1,), [whole(parts)], whole(shape), shape, [], (), [parts], 0, later_than=later_than)


def place_down(store, refs, half, back, scalars, at):
    y_size = len(back)
    for n, ref in enumerate(refs):
        g, s = divmod(n, y_size)
        row = pl.multiple_of(scalars[at + s] * half, half) + g * y_size * half
        store[pl.ds(row, half), :] = ref[0]


def projected_first_kernel(count, blocks, tok_ref, *refs):
    out_ref = refs[-1]
    down = jnp.concatenate([r[...] for r in refs[:count]], axis=0)

    @pl.when(pl.program_id(0) == 0)
    def _():
        out_ref[...] = jnp.zeros_like(out_ref)

    out_ref[...] += lax.dot_general(tok_ref[...], down, nt, preferred_element_type=f32)


def projected_first(tokens, downs, blocks, rows):
    group, cols = downs[0].shape
    total = group * len(downs)
    bc = column_block(cols)
    per = cols // bc
    return call(
        functools.partial(projected_first_kernel, len(downs)),
        "projected_own",
        (per,),
        [column_spec(rows, cols, lambda j, b: (b[0], j))]
        + [pl.BlockSpec((group, bc), lambda j, b: (0, j)) for _ in downs],
        pl.BlockSpec((rows, total), lambda j, b: (0, 0)),
        jax.ShapeDtypeStruct((rows, total), f32),
        [],
        (blocks,),
        [tokens, *downs],
        2 * rows * cols * total,
        in_hbm=(0,),
    )


def projected_kernel(pieces, y_size, half, tiles, rank, split, scalars, first, policy, tok_ref, base_ref, masked_ref, *refs):
    piece_refs, (send_ref, keep_ref, store, total) = refs[:pieces], refs[pieces:]
    step = pl.program_id(0) * pl.num_programs(1) + pl.program_id(1)

    @pl.when(step == 0)
    def _():
        total[...] = base_ref[...]

    place_down(store, piece_refs, half, range(y_size), scalars, 0)
    total[...] += lax.dot_general(tok_ref[...], store[...], nt, preferred_element_type=f32)

    @pl.when(step == pl.num_programs(0) * pl.num_programs(1) - 1)
    def _():
        count = pieces // y_size
        columns = columns_policy(first, count, half * y_size, rank)
        tile_rows = total.shape[0] // tiles
        chosen = []
        for i in range(tiles):
            part = total[i * tile_rows : (i + 1) * tile_rows, :]
            chosen.append(jnp.where(columns == policy[i], part, 0.0).T)
        projected = jnp.concatenate(chosen, axis=1).astype(bf16)
        value = jnp.dot(projected, masked_ref[...], preferred_element_type=f32)
        keep_ref[...] = value[:split]
        send_ref[...] = value[split:]


def projected_call(scalars, first, policy, blocks_at, tokens, base, masked, pieces, y_size, half, rank, split):
    rows, kv = masked.shape
    steps, _, cols = pieces[0].shape
    total = half * len(pieces)
    bc = column_block(cols)
    per = cols // bc
    return call(
        functools.partial(projected_kernel, len(pieces), y_size, half, policy.shape[0], rank, split),
        "projected",
        (steps, per),
        [
            column_spec(rows, cols, lambda i, j, s, *_: (s[blocks_at + i], j)),
            whole(base),
            whole(masked),
        ]
        + [pl.BlockSpec((1, half, bc), lambda i, j, *_: (i, 0, j)) for _ in pieces],
        [
            pl.BlockSpec((total - split, kv), lambda *_: (0, 0)),
            pl.BlockSpec((split, kv), lambda *_: (0, 0)),
        ],
        [jax.ShapeDtypeStruct((total - split, kv), f32), jax.ShapeDtypeStruct((split, kv), f32)],
        [pltpu.VMEM((total, bc), bf16), pltpu.VMEM((rows, total), f32)],
        (scalars, first, policy),
        [tokens, base, masked, *pieces],
        2 * rows * cols * steps * total + 2 * rows * kv * total,
        in_hbm=(0,),
    )


def input_kernel(views, pieces, y_size, half, has_out, scalars, low_ref, *refs):
    masked_refs, refs = refs[:views], refs[views:]
    weight_refs, refs = refs[:views], refs[views:]
    down_refs, refs = refs[:pieces], refs[pieces:]
    if has_out:
        refs = refs[1:]
    out_ref = refs[0]
    masked = jnp.concatenate([r[...] for r in masked_refs], axis=1)
    weight = jnp.concatenate([r[...] for r in weight_refs], axis=1)
    value = lax.dot_general(masked, weight, nt, preferred_element_type=f32)
    if y_size:
        place_down(refs[1], down_refs, half, range(y_size), scalars, 1 + views)
        down = refs[1][...]
    else:
        down = jnp.concatenate([r[...] for r in down_refs], axis=0)
    value = value + jnp.dot(low_ref[...], down, preferred_element_type=f32)
    out_ref[...] = value.astype(bf16)


def input_call(scalars, low, masked, weights, downs, step, y_size, out, width, last=False, later_than=()):
    rows, kv = masked.shape
    cols = weights[0].shape[0]
    depth = weights[0].shape[1]
    half = downs[0].shape[-2]
    total = low.shape[1]
    bc = column_block(cols)
    per = cols // bc
    if y_size:
        down_specs = [pl.BlockSpec((1, half, bc), lambda j, s: (step, 0, j)) for _ in downs]
    else:
        down_specs = [pl.BlockSpec((half, bc), lambda j, s: (0, j)) for _ in downs]
    in_specs = [whole(low)]
    for v in range(len(weights)):
        in_specs.append(pl.BlockSpec((rows, depth), functools.partial(lambda v, j, s: (0, s[1 + v]), v)))
    in_specs += [pl.BlockSpec((bc, depth), lambda j, s: (j, 0)) for _ in weights] + down_specs
    args = [low] + [masked] * len(weights) + list(weights) + list(downs)
    aliases = {}
    if out is not None:
        in_specs.append(pl.BlockSpec(memory_space=pl.ANY))
        aliases = {1 + len(args): 0}
        args.append(out)
    return call(
        functools.partial(input_kernel, len(weights), len(downs), y_size, half, out is not None),
        "input_cotangent",
        (per,),
        in_specs,
        column_spec(rows, cols, lambda j, s: (s[0], j)),
        jax.ShapeDtypeStruct((rows, width) if cols % 128 == 0 else (width // cols, rows, cols), bf16),
        [pltpu.VMEM((total, bc), bf16)] if y_size else [],
        (scalars,),
        args,
        2 * rows * cols * (kv + total),
        aliases,
        (1 + len(weights),) if not y_size else range(1 + 2 * len(weights), 1 + 2 * len(weights) + len(downs)) if last else (),
        later_than,
    )


def body(tokens, value_cotangent, value_weight, adapter_down, adapter_up, tile_token_policy, tile_live_length):
    y_size, x_size, c_size, z_size = (lax.axis_size(a) for a in ("league", "x", "core", "fsdp"))
    y, x, c, z = (lax.axis_index(a) for a in ("league", "x", "core", "fsdp"))
    rows, width = tokens.shape
    kv = value_cotangent.shape[1]
    own_policies, rank, cols = adapter_down.shape
    group = own_policies * rank
    half = group // y_size
    depth = kv // (y_size * c_size)

    def ints(*values):
        return jnp.stack([jnp.asarray(v, jnp.int32) for v in values])

    up_x = gather_steps(adapter_up.reshape(group, kv), "x")
    ups = [piece for s in zip(*[gather_steps(u, "core") for u in up_x]) for piece in s]
    groups = [(dc, dx) for dc in range(c_size) for dx in range(x_size)]
    first = ints(*[(((x - dx) % x_size) * c_size + (c - dc) % c_size) * own_policies for dc, dx in groups])

    own_down = adapter_down.reshape(group, cols)
    down_x = gather_steps(own_down, "x")
    own_downs = [piece for s in zip(*[gather_steps(u, "core") for u in down_x]) for piece in s]
    down_half = lax.dynamic_slice_in_dim(own_down, y * half, half, 0)
    down_z = jnp.stack([shift(down_half, "fsdp", s) for s in range(1, z_size)])
    down_pieces = {}
    for dx, piece in enumerate(gather_steps(down_z, "x")):
        for dy, got in enumerate(gather_steps(piece, "league")):
            for dc, last in enumerate(gather_steps(got, "core")):
                down_pieces[dc, dx, dy] = last
    downs = [down_pieces[dc, dx, dy] for dc, dx in groups for dy in range(y_size)]
    league_back = [(y - s) % y_size for s in range(y_size)]

    masked, low, low_t = low_rank_call(first, tile_token_policy, tile_live_length, value_cotangent, ups, rank)

    tokens = by_owner(tokens, cols)

    split = x_size * group
    normalizer = 1.0 / math.sqrt(rows * x_size * c_size * z_size)
    order = [(z + s) % z_size for s in range(z_size)]
    chunks = [list(range(z_size // 2, z_size)), list(range(z_size // 2))]
    over_x = []
    for chunk in chunks:
        places = ints(*[order[s] for s in chunk])
        sent = [
            shift(partial_call(low_t, s * split, split, tokens, places, cols, None, [bf16])[0], "core", -s)
            for s in range(1, c_size)
        ]
        added = sent[0] if len(sent) == 1 else sum(v.astype(f32) for v in sent)
        kept, *for_x = partial_call(low_t, 0, split, tokens, places, cols, added, [f32] + [bf16] * (x_size - 1))
        for_x = [shift(v, "x", -s - 1) for s, v in enumerate(for_x)]
        over_x.append((kept, for_x))

    blocks = ints(*[(z - s) % z_size for s in range(z_size)])
    base = projected_first(tokens, own_downs, blocks, rows)
    scalars = jnp.concatenate([ints(*league_back), blocks[1:]])
    sent_b, kept_b = projected_call(
        scalars, first, tile_token_policy, y_size, tokens, base, masked, downs, y_size, half, rank, split
    )
    got_b = [shift(sent_b[(s - 1) * split : s * split], "core", -s) for s in range(1, c_size)]
    x_at = ints(*[(x - s) % x_size for s in range(x_size)])
    own_b = spread_call(x_at, kept_b, got_b, group, z_size)
    own_b = own_b.reshape((x_size * z_size,) + own_b.shape[2:])
    parts_b = lax.all_to_all(own_b, ("x", "fsdp"), split_axis=0, concat_axis=0, tiled=True)
    share_b = share_call(parts_b, adapter_scale * normalizer, z_size)
    grad_b = lax.all_to_all(share_b, "fsdp", split_axis=0, concat_axis=0, tiled=True).astype(f32)

    got_a, early = [], []
    for chunk, (kept, for_x), before in zip(chunks, over_x, (own_b, share_b)):
        parts = settle_call(kept, for_x, [bf16 if s else f32 for s in chunk], [before])
        early = early or list(parts[:1])
        got_a += [shift(v, "fsdp", s).astype(f32) if s else v for s, v in zip(chunk, parts)]
    grad_a = sum(got_a[1:], got_a[0]) * normalizer

    out = input_call(ints(z, 0), low, masked, [value_weight], own_downs, 0, 0, None, width)
    held = lax.dynamic_slice_in_dim(value_weight, (y * c_size + c) * depth, depth, 1)
    for s in range(1, z_size):
        held = shift(held, "fsdp", 1)
        weights, places = [], []
        for dy, piece in enumerate(gather_steps(held, "league")):
            for dc, got in enumerate(gather_steps(piece, "core")):
                weights.append(got)
                places.append(league_back[dy] * c_size + (c - dc) % c_size)
        out = input_call(
            ints((z - s) % z_size, *places, *league_back), low, masked, weights, downs, s - 1, y_size, out, width,
            later_than=early if s == z_size - 2 else (),
            last=s >= z_size - 2,
        )
    if cols % 128:
        out = out.swapaxes(0, 1).reshape(rows, width)
    return out, grad_a.reshape(own_policies, rank, cols), grad_b.reshape(own_policies, rank, kv)


def solution(mesh):
    league, dp, fsdp = mesh.devices.shape
    fine = Mesh(mesh.devices.reshape(league, dp // cores, cores, fsdp), ("league", "x", "core", "fsdp"))
    every = ("league", "x", "core", "fsdp")
    return jax.shard_map(
        body,
        mesh=fine,
        in_specs=(
            P(every, None),
            P(every, None),
            P("fsdp", None),
            P(("x", "core"), None, "fsdp"),
            P(("x", "core"), None, None),
            P(every),
            P(every),
        ),
        out_specs=(
            P(every, None),
            P(("league", "x", "core"), None, "fsdp"),
            P(("league", "x", "core"), None, None),
        ),
        check_vma=False,
    )
```

```python
import functools
import math

import jax
import jax.numpy as jnp
from jax import lax
from jax.experimental import pallas as pl
from jax.experimental.pallas import tpu as pltpu
from jax.sharding import Mesh
from jax.sharding import PartitionSpec as P

adapter_scale = 2.0
cores = 2
bf16, f32 = jnp.bfloat16, jnp.float32
vmem_bytes = 16 * 1024 * 1024
cost_factor = 20
nt = (((1,), (1,)), ((), ()))


def shift(value, axis, by):
    size = lax.axis_size(axis)
    return lax.ppermute(value, axis, [(i, (i + by) % size) for i in range(size)])


def gather_steps(value, axis):
    blocks = [value]
    for _ in range(lax.axis_size(axis) - 1):
        blocks.append(shift(blocks[-1], axis, 1))
    return blocks


def column_block(cols):
    for size in (640, 512, 384, 256, 128):
        if cols % size == 0:
            return size
    return cols


def column_spec(rows, cols, place):
    bc = column_block(cols)
    per = cols // bc
    if cols % 128 == 0:
        def index(*at):
            owner, block = place(*at)
            return 0, owner * per + block

        return pl.BlockSpec((rows, bc), index)

    def index(*at):
        owner, block = place(*at)
        return owner, 0, block

    return pl.BlockSpec((None, rows, bc), index)


def by_owner(value, cols):
    if cols % 128 == 0:
        return value
    return value.reshape(value.shape[0], -1, cols).swapaxes(0, 1)


def call(kernel, name, grid, in_specs, out_specs, out_shape, scratch, scalars, args, flops, aliases=None, in_hbm=(), later_than=()):
    args = [pltpu.with_memory_space_constraint(a, pltpu.HBM) if n in in_hbm else a for n, a in enumerate(args)]
    moved = sum(math.prod(a.shape) * a.dtype.itemsize for a in args)
    count, extra = len(scalars) + len(args), len(later_than)
    return pl.pallas_call(
        lambda *refs: kernel(*refs[:count], *refs[count + extra :]),
        grid_spec=pltpu.PrefetchScalarGridSpec(
            num_scalar_prefetch=len(scalars), grid=grid, in_specs=in_specs + [pl.BlockSpec(memory_space=pl.ANY)] * extra, out_specs=out_specs, scratch_shapes=scratch
        ),
        out_shape=out_shape,
        compiler_params=pltpu.CompilerParams(vmem_limit_bytes=vmem_bytes),
        cost_estimate=pl.CostEstimate(flops=cost_factor * flops, bytes_accessed=cost_factor * moved, transcendentals=0),
        input_output_aliases=aliases or {},
        name=name,
    )(*scalars, *args, *later_than)


def whole(array):
    zeros = (0,) * array.ndim
    return pl.BlockSpec(array.shape, lambda *_: zeros)


def columns_policy(first, count, group, rank):
    parts = []
    for g in range(count):
        parts.append(first[g] + lax.broadcasted_iota(jnp.int32, (1, group), 1) // rank)
    return jnp.concatenate(parts, axis=1)


def low_rank_kernel(count, group, rank, first, policy, live, cot_ref, *refs):
    up_refs, (masked_ref, low_ref, low_t_ref) = refs[:count], refs[count:]
    tile = pl.program_id(0)
    rows, kv = cot_ref.shape
    keep = lax.broadcasted_iota(jnp.int32, (rows, kv), 0) < live[tile]
    masked = jnp.where(keep, cot_ref[...].astype(f32), 0.0).astype(bf16)
    masked_ref[...] = masked
    up = jnp.concatenate([r[...] for r in up_refs], axis=0)
    low = adapter_scale * lax.dot_general(masked, up, nt, preferred_element_type=f32)
    mine = columns_policy(first, count, group, rank) == policy[tile]
    low = jnp.where(mine, low, 0.0)
    low_ref[...] = low.astype(bf16)
    low_t_ref[...] = low.T.astype(bf16)


def low_rank_call(first, policy, live, cotangent, ups, rank):
    rows, kv = cotangent.shape
    tiles = policy.shape[0]
    group = ups[0].shape[0]
    total = group * len(ups)
    tile_rows = rows // tiles
    return call(
        functools.partial(low_rank_kernel, len(ups), group, rank),
        "low_rank",
        (tiles,),
        [pl.BlockSpec((tile_rows, kv), lambda i, *_: (i, 0))] + [whole(u) for u in ups],
        [
            pl.BlockSpec((tile_rows, kv), lambda i, *_: (i, 0)),
            pl.BlockSpec((tile_rows, total), lambda i, *_: (i, 0)),
            pl.BlockSpec((total, tile_rows), lambda i, *_: (0, i)),
        ],
        [
            jax.ShapeDtypeStruct((rows, kv), bf16),
            jax.ShapeDtypeStruct((rows, total), bf16),
            jax.ShapeDtypeStruct((total, rows), bf16),
        ],
        [],
        (first, policy, live),
        [cotangent, *ups],
        2 * rows * kv * total,
        in_hbm=(0,),
    )


def partial_kernel(adds, low_t_ref, tok_ref, *refs):
    value = jnp.dot(low_t_ref[...], tok_ref[...], preferred_element_type=f32)
    if adds:
        value = value + refs[0][0].astype(f32)
    at = 0
    for ref in refs[adds:]:
        ref[0] = value[at : at + ref.shape[1]].astype(ref.dtype)
        at += ref.shape[1]


def partial_call(low_t, first, rows, tokens, blocks, cols, added, kinds):
    count = blocks.shape[0]
    bc = column_block(cols)
    per = cols // bc
    depth = low_t.shape[1]
    in_specs = [
        pl.BlockSpec((rows, depth), lambda i, j, b: (first // rows, 0)),
        column_spec(depth, cols, lambda i, j, b: (b[i], j)),
    ]
    args = [low_t, tokens]
    if added is not None:
        in_specs.append(pl.BlockSpec((1, rows, bc), lambda i, j, b: (i, 0, j)))
        args.append(added)
    part = rows // len(kinds)
    return call(
        lambda b, *refs: partial_kernel(int(added is not None), *refs),
        "down_partial",
        (count, per),
        in_specs,
        [pl.BlockSpec((1, part, bc), lambda i, j, b: (i, 0, j)) for _ in kinds],
        [jax.ShapeDtypeStruct((count, part, cols), kind) for kind in kinds],
        [],
        (blocks,),
        args,
        2 * rows * depth * cols * count,
        in_hbm=(1,),
    )


def settle_kernel(kept_ref, *refs):
    count = kept_ref.shape[0]
    got_refs, out_refs = refs[:-count], refs[-count:]
    for m, out_ref in enumerate(out_refs):
        value = kept_ref[m]
        for ref in got_refs:
            value = value + ref[m].astype(f32)
        out_ref[...] = value.astype(out_ref.dtype)


def settle_call(kept, got, kinds, later_than):
    shapes = [jax.ShapeDtypeStruct(kept.shape[1:], kind) for kind in kinds]
    args = [kept, *got]
    specs = [whole(v) for v in args]
    outs = [whole(v) for v in shapes]
    return call(settle_kernel, "settle", (1,), specs, outs, shapes, [], (), args, 0, later_than=later_than)


def spread_kernel(group, x_at, kept_ref, *refs):
    out_ref = refs[-1]
    chunk = out_ref.shape[2]
    for s in range(out_ref.shape[0]):
        for m in range(out_ref.shape[1]):
            here = slice(s * group + m * chunk, s * group + (m + 1) * chunk)
            value = kept_ref[here, :]
            for ref in refs[:-1]:
                value = value + ref[here, :]
            out_ref[x_at[s], m] = value.astype(bf16)


def spread_call(x_at, kept, got, group, z_size):
    rows, kv = kept.shape
    shape = jax.ShapeDtypeStruct((rows // group, z_size, group // z_size, kv), bf16)
    args = [kept, *got]
    kernel = functools.partial(spread_kernel, group)
    return call(kernel, "spread", (1,), [whole(v) for v in args], whole(shape), shape, [], (x_at,), args, 0)


def share_kernel(scale, parts_ref, out_ref):
    value = parts_ref[0].astype(f32)
    for n in range(1, parts_ref.shape[0]):
        value = value + parts_ref[n].astype(f32)
    value = (value * scale).astype(bf16)
    for n in range(out_ref.shape[0]):
        out_ref[n] = value


def share_call(parts, scale, copies, later_than=()):
    shape = jax.ShapeDtypeStruct((copies,) + parts.shape[1:], bf16)
    kernel = functools.partial(share_kernel, scale)
    return call(kernel, "share", (1,), [whole(parts)], whole(shape), shape, [], (), [parts], 0, later_than=later_than)


def place_down(store, refs, half, back, scalars, at):
    y_size = len(back)
    for n, ref in enumerate(refs):
        g, s = divmod(n, y_size)
        row = pl.multiple_of(scalars[at + s] * half, half) + g * y_size * half
        store[pl.ds(row, half), :] = ref[0]


def projected_first_kernel(count, blocks, tok_ref, *refs):
    out_ref = refs[-1]
    down = jnp.concatenate([r[...] for r in refs[:count]], axis=0)

    @pl.when(pl.program_id(0) == 0)
    def _():
        out_ref[...] = jnp.zeros_like(out_ref)

    out_ref[...] += lax.dot_general(tok_ref[...], down, nt, preferred_element_type=f32)


def projected_first(tokens, downs, blocks, rows):
    group, cols = downs[0].shape
    total = group * len(downs)
    bc = column_block(cols)
    per = cols // bc
    return call(
        functools.partial(projected_first_kernel, len(downs)),
        "projected_own",
        (per,),
        [column_spec(rows, cols, lambda j, b: (b[0], j))]
        + [pl.BlockSpec((group, bc), lambda j, b: (0, j)) for _ in downs],
        pl.BlockSpec((rows, total), lambda j, b: (0, 0)),
        jax.ShapeDtypeStruct((rows, total), f32),
        [],
        (blocks,),
        [tokens, *downs],
        2 * rows * cols * total,
        in_hbm=(0,),
    )


def projected_kernel(pieces, y_size, half, tiles, rank, split, scalars, first, policy, tok_ref, base_ref, masked_ref, *refs):
    piece_refs, (send_ref, keep_ref, store, total) = refs[:pieces], refs[pieces:]
    step = pl.program_id(0) * pl.num_programs(1) + pl.program_id(1)

    @pl.when(step == 0)
    def _():
        total[...] = base_ref[...]

    place_down(store, piece_refs, half, range(y_size), scalars, 0)
    total[...] += lax.dot_general(tok_ref[...], store[...], nt, preferred_element_type=f32)

    @pl.when(step == pl.num_programs(0) * pl.num_programs(1) - 1)
    def _():
        count = pieces // y_size
        columns = columns_policy(first, count, half * y_size, rank)
        tile_rows = total.shape[0] // tiles
        chosen = []
        for i in range(tiles):
            part = total[i * tile_rows : (i + 1) * tile_rows, :]
            chosen.append(jnp.where(columns == policy[i], part, 0.0).T)
        projected = jnp.concatenate(chosen, axis=1).astype(bf16)
        value = jnp.dot(projected, masked_ref[...], preferred_element_type=f32)
        keep_ref[...] = value[:split]
        send_ref[...] = value[split:]


def projected_call(scalars, first, policy, blocks_at, tokens, base, masked, pieces, y_size, half, rank, split):
    rows, kv = masked.shape
    steps, _, cols = pieces[0].shape
    total = half * len(pieces)
    bc = column_block(cols)
    per = cols // bc
    return call(
        functools.partial(projected_kernel, len(pieces), y_size, half, policy.shape[0], rank, split),
        "projected",
        (steps, per),
        [
            column_spec(rows, cols, lambda i, j, s, *_: (s[blocks_at + i], j)),
            whole(base),
            whole(masked),
        ]
        + [pl.BlockSpec((1, half, bc), lambda i, j, *_: (i, 0, j)) for _ in pieces],
        [
            pl.BlockSpec((total - split, kv), lambda *_: (0, 0)),
            pl.BlockSpec((split, kv), lambda *_: (0, 0)),
        ],
        [jax.ShapeDtypeStruct((total - split, kv), f32), jax.ShapeDtypeStruct((split, kv), f32)],
        [pltpu.VMEM((total, bc), bf16), pltpu.VMEM((rows, total), f32)],
        (scalars, first, policy),
        [tokens, base, masked, *pieces],
        2 * rows * cols * steps * total + 2 * rows * kv * total,
        in_hbm=(0,),
    )


def input_kernel(views, pieces, y_size, half, has_out, scalars, low_ref, *refs):
    masked_refs, refs = refs[:views], refs[views:]
    weight_refs, refs = refs[:views], refs[views:]
    down_refs, refs = refs[:pieces], refs[pieces:]
    if has_out:
        refs = refs[1:]
    out_ref = refs[0]
    masked = jnp.concatenate([r[...] for r in masked_refs], axis=1)
    weight = jnp.concatenate([r[...] for r in weight_refs], axis=1)
    value = lax.dot_general(masked, weight, nt, preferred_element_type=f32)
    if y_size:
        place_down(refs[1], down_refs, half, range(y_size), scalars, 1 + views)
        down = refs[1][...]
    else:
        down = jnp.concatenate([r[...] for r in down_refs], axis=0)
    value = value + jnp.dot(low_ref[...], down, preferred_element_type=f32)
    out_ref[...] = value.astype(bf16)


def input_call(scalars, low, masked, weights, downs, step, y_size, out, width, last=False, later_than=()):
    rows, kv = masked.shape
    cols = weights[0].shape[0]
    depth = weights[0].shape[1]
    half = downs[0].shape[-2]
    total = low.shape[1]
    bc = column_block(cols)
    per = cols // bc
    if y_size:
        down_specs = [pl.BlockSpec((1, half, bc), lambda j, s: (step, 0, j)) for _ in downs]
    else:
        down_specs = [pl.BlockSpec((half, bc), lambda j, s: (0, j)) for _ in downs]
    in_specs = [whole(low)]
    for v in range(len(weights)):
        in_specs.append(pl.BlockSpec((rows, depth), functools.partial(lambda v, j, s: (0, s[1 + v]), v)))
    in_specs += [pl.BlockSpec((bc, depth), lambda j, s: (j, 0)) for _ in weights] + down_specs
    args = [low] + [masked] * len(weights) + list(weights) + list(downs)
    aliases = {}
    if out is not None:
        in_specs.append(pl.BlockSpec(memory_space=pl.ANY))
        aliases = {1 + len(args): 0}
        args.append(out)
    return call(
        functools.partial(input_kernel, len(weights), len(downs), y_size, half, out is not None),
        "input_cotangent",
        (per,),
        in_specs,
        column_spec(rows, cols, lambda j, s: (s[0], j)),
        jax.ShapeDtypeStruct((rows, width) if cols % 128 == 0 else (width // cols, rows, cols), bf16),
        [pltpu.VMEM((total, bc), bf16)] if y_size else [],
        (scalars,),
        args,
        2 * rows * cols * (kv + total),
        aliases,
        (1 + len(weights),) if not y_size else range(1 + 2 * len(weights), 1 + 2 * len(weights) + len(downs)) if last else (),
        later_than,
    )


def body(tokens, value_cotangent, value_weight, adapter_down, adapter_up, tile_token_policy, tile_live_length):
    y_size, x_size, c_size, z_size = (lax.axis_size(a) for a in ("league", "x", "core", "fsdp"))
    y, x, c, z = (lax.axis_index(a) for a in ("league", "x", "core", "fsdp"))
    rows, width = tokens.shape
    kv = value_cotangent.shape[1]
    own_policies, rank, cols = adapter_down.shape
    group = own_policies * rank
    half = group // y_size
    depth = kv // (y_size * c_size)

    def ints(*values):
        return jnp.stack([jnp.asarray(v, jnp.int32) for v in values])

    up_x = gather_steps(adapter_up.reshape(group, kv), "x")
    ups = [piece for s in zip(*[gather_steps(u, "core") for u in up_x]) for piece in s]
    groups = [(dc, dx) for dc in range(c_size) for dx in range(x_size)]
    first = ints(*[(((x - dx) % x_size) * c_size + (c - dc) % c_size) * own_policies for dc, dx in groups])

    own_down = adapter_down.reshape(group, cols)
    down_x = gather_steps(own_down, "x")
    own_downs = [piece for s in zip(*[gather_steps(u, "core") for u in down_x]) for piece in s]
    down_half = lax.dynamic_slice_in_dim(own_down, y * half, half, 0)
    down_z = jnp.stack([shift(down_half, "fsdp", s) for s in range(1, z_size)])
    down_pieces = {}
    for dx, piece in enumerate(gather_steps(down_z, "x")):
        for dy, got in enumerate(gather_steps(piece, "league")):
            for dc, last in enumerate(gather_steps(got, "core")):
                down_pieces[dc, dx, dy] = last
    downs = [down_pieces[dc, dx, dy] for dc, dx in groups for dy in range(y_size)]
    league_back = [(y - s) % y_size for s in range(y_size)]

    masked, low, low_t = low_rank_call(first, tile_token_policy, tile_live_length, value_cotangent, ups, rank)

    tokens = by_owner(tokens, cols)

    split = x_size * group
    normalizer = 1.0 / math.sqrt(rows * x_size * c_size * z_size)
    order = [(z + s) % z_size for s in range(z_size)]
    chunks = [list(range(z_size // 2, z_size)), list(range(z_size // 2))]
    over_x = []
    for chunk in chunks:
        places = ints(*[order[s] for s in chunk])
        sent = [
            shift(partial_call(low_t, s * split, split, tokens, places, cols, None, [bf16])[0], "core", -s)
            for s in range(1, c_size)
        ]
        added = sent[0] if len(sent) == 1 else sum(v.astype(f32) for v in sent)
        kept, *for_x = partial_call(low_t, 0, split, tokens, places, cols, added, [f32] + [bf16] * (x_size - 1))
        for_x = [shift(v, "x", -s - 1) for s, v in enumerate(for_x)]
        over_x.append((kept, for_x))

    blocks = ints(*[(z - s) % z_size for s in range(z_size)])
    base = projected_first(tokens, own_downs, blocks, rows)
    scalars = jnp.concatenate([ints(*league_back), blocks[1:]])
    sent_b, kept_b = projected_call(
        scalars, first, tile_token_policy, y_size, tokens, base, masked, downs, y_size, half, rank, split
    )
    got_b = [shift(sent_b[(s - 1) * split : s * split], "core", -s) for s in range(1, c_size)]
    x_at = ints(*[(x - s) % x_size for s in range(x_size)])
    own_b = spread_call(x_at, kept_b, got_b, group, z_size)
    own_b = own_b.reshape((x_size * z_size,) + own_b.shape[2:])
    parts_b = lax.all_to_all(own_b, ("x", "fsdp"), split_axis=0, concat_axis=0, tiled=True)
    share_b = share_call(parts_b, adapter_scale * normalizer, z_size)
    grad_b = lax.all_to_all(share_b, "fsdp", split_axis=0, concat_axis=0, tiled=True).astype(f32)

    got_a, early = [], []
    for chunk, (kept, for_x), before in zip(chunks, over_x, (own_b, share_b)):
        parts = settle_call(kept, for_x, [bf16 if s else f32 for s in chunk], [before])
        early = early or list(parts[:1])
        got_a += [shift(v, "fsdp", s).astype(f32) if s else v for s, v in zip(chunk, parts)]
    grad_a = sum(got_a[1:], got_a[0]) * normalizer

    out = input_call(ints(z, 0), low, masked, [value_weight], own_downs, 0, 0, None, width)
    held = lax.dynamic_slice_in_dim(value_weight, (y * c_size + c) * depth, depth, 1)
    for s in range(1, z_size):
        held = shift(held, "fsdp", 1)
        weights, places = [], []
        for dy, piece in enumerate(gather_steps(held, "league")):
            for dc, got in enumerate(gather_steps(piece, "core")):
                weights.append(got)
                places.append(league_back[dy] * c_size + (c - dc) % c_size)
        out = input_call(
            ints((z - s) % z_size, *places, *league_back), low, masked, weights, downs, s - 1, y_size, out, width,
            later_than=early if s == z_size - 2 else [own_b] if s == 1 else (),
            last=s >= z_size - 2,
        )
    if cols % 128:
        out = out.swapaxes(0, 1).reshape(rows, width)
    return out, grad_a.reshape(own_policies, rank, cols), grad_b.reshape(own_policies, rank, kv)


def solution(mesh):
    league, dp, fsdp = mesh.devices.shape
    fine = Mesh(mesh.devices.reshape(league, dp // cores, cores, fsdp), ("league", "x", "core", "fsdp"))
    every = ("league", "x", "core", "fsdp")
    return jax.shard_map(
        body,
        mesh=fine,
        in_specs=(
            P(every, None),
            P(every, None),
            P("fsdp", None),
            P(("x", "core"), None, "fsdp"),
            P(("x", "core"), None, None),
            P(every),
            P(every),
        ),
        out_specs=(
            P(every, None),
            P(("league", "x", "core"), None, "fsdp"),
            P(("league", "x", "core"), None, None),
        ),
        check_vma=False,
    )
```
